256 devices in a mesh: op: 8 (over x, y_lo), str: 32 (over z, y_hi, core).
Axes of the slice: x: 4, y: 4 (y_hi: 2, y_lo: 2; y = y_hi * 2 + y_lo), z: 8, core: 2. Of those that a mesh axis runs over, the one named last changes fastest.
Arguments:
- coeffs: float32 [4096, 4096], P('str'), may hold values from -6 to 6
- previous: float32 [4096, 4096], P('str'), may hold values from -6 to 6
- block_values: bfloat16 [8, 32, 6, 128, 128], P('op'), may hold values from -0.21875 to 0.21875
- block_cols: int32 [8, 32, 6], P('op'), may hold values from 0 to 31, as said below
Outputs:
- advanced: float32 [4096, 4096], P('str')
The draws below stay inside these ranges and needn't reach their ends.
Inputs may be any that keep to these rules, and one draw needn't show every extreme that they name: For every term k and block row r, block_cols[k, r, 0] equals r and the 6 entries of block_cols[k, r] are distinct.
All inputs are finite; a program needn't handle non-finite values.
Results may differ from the reference program's by a relative error of at most 0.0003.
Values sent between devices are 32-bit elements; how exact they have to be, the bound alone decides.
No kernel may reach another device: no remote copies, remote signals or barrier semaphores. Data moves between devices by JAX's collectives and lax.ppermute only.
A program may use at most 128 MiB of HBM per device.

```python
import math
import jax
import jax.numpy as jnp
from jax import lax

STRINGS = 4096
BLOCK = 128
BLOCKS = 32
ROW_BLOCKS = 6
TERMS = 8
STEPS = 2


def draw_block_cols(key, part):
    row_keys = jax.random.split(key, TERMS * BLOCKS)

    def one_row(row_key):
        return jax.random.permutation(row_key, BLOCKS - 1)[:ROW_BLOCKS - 1].astype(jnp.int32)
    others = jax.vmap(one_row)(row_keys).reshape(TERMS, BLOCKS, ROW_BLOCKS - 1)
    block_rows = jnp.arange(BLOCKS, dtype=jnp.int32)[None, :, None]
    others = (block_rows + 1 + others) % BLOCKS
    diagonal = jnp.broadcast_to(block_rows, (TERMS, BLOCKS, 1))
    return jnp.concatenate([diagonal, others], axis=2).astype(jnp.int32)


def shard_levels(rng, extent, shards, smallest, top_value):
    gain, own = 1.0, jax.random.fold_in(rng, 6)
    for dim, parts in shards:
        steps = jnp.exp(jax.random.uniform(jax.random.fold_in(own, dim), (parts,), jnp.float32, smallest / len(shards), top_value / len(shards)))
        gain = gain * jnp.repeat(steps, extent[dim] // parts).reshape([-1 if axis == dim else 1 for axis in range(len(extent))])
    return gain


def bell_draw(rng, extent, scale, most, pieces=(), held_as=jnp.bfloat16):
    gain = shard_levels(rng, extent, pieces, -0.22, 0.18) if pieces else 1.0
    drawn = jax.random.normal(rng, extent, jnp.float32) * scale * gain
    return jnp.minimum(jnp.maximum(drawn, -most), most).astype(held_as)


def setup_inputs(seed: int = 0) -> dict:
    arg_keys = jax.random.split(jax.random.key(seed), 5)
    return {
        "coeffs": bell_draw(arg_keys[0], (STRINGS, STRINGS), 1.0, 6.0, ((0, 32),), jnp.float32),
        "previous": bell_draw(arg_keys[1], (STRINGS, STRINGS), 1.0, 6.0, ((0, 32),), jnp.float32),
        "block_values": bell_draw(arg_keys[2], (TERMS, BLOCKS, ROW_BLOCKS, BLOCK, BLOCK), (ROW_BLOCKS * BLOCK) ** -0.5, 0.21875, ((0, 8),)),
        "block_cols": draw_block_cols(jax.random.fold_in(arg_keys[4], 71), 0),
    }


def apply_term(field, values, columns):
    factors = values.astype(jnp.float32)
    column_list = columns.reshape(-1)
    gathered = jnp.take(field.reshape(STRINGS, BLOCKS, BLOCK), column_list, axis=1)
    gathered = gathered.reshape(STRINGS, BLOCKS, ROW_BLOCKS, BLOCK)
    beta_side = jnp.einsum('arjc,rjoc->aro', gathered, factors, precision=lax.Precision.HIGHEST)
    beta_side = beta_side.reshape(STRINGS, STRINGS)
    grouped = jnp.take(beta_side.reshape(BLOCKS, BLOCK, STRINGS), column_list, axis=0)
    grouped = grouped.reshape(BLOCKS, ROW_BLOCKS, BLOCK, STRINGS)
    alpha_side = jnp.einsum('rjoc,rjcb->rob', factors, grouped, precision=lax.Precision.HIGHEST)
    return alpha_side.reshape(STRINGS, STRINGS)

def sigma_all(field, block_values, block_cols):

    def add_term(summed, term_pair):
        return (summed + apply_term(field, term_pair[0], term_pair[1]), None)
    summed, unused = lax.scan(add_term, jnp.zeros((STRINGS, STRINGS), jnp.float32), (block_values, block_cols))
    return summed

def reference(coeffs, previous, block_values, block_cols):
    step_scale = 2.0 / math.sqrt(TERMS)
    earlier, current = (previous, coeffs)
    for step_index in range(STEPS):
        updated = step_scale * sigma_all(current, block_values, block_cols) - earlier
        earlier, current = (current, updated)
    return current
```

```python
import functools
import math

import jax
import jax.numpy as jnp
from jax import lax
from jax.experimental import pallas as pl
from jax.experimental.pallas import tpu as pltpu
from jax.sharding import PartitionSpec as P

BLOCK = 128
CHUNKS = 2
ROWS_PER_STEP = 8


def split(values):
    high = values.astype(jnp.bfloat16)
    return high, (values - high.astype(jnp.float32)).astype(jnp.bfloat16)


def side_kernel(cols, *refs, blocked_in, turned_in, turned_out, rows, slots, per_step):
    field_count = len(turned_in) if turned_in else 1
    fields, factors, outs, halves = refs[:field_count], refs[field_count], refs[field_count + 1 : -1], refs[-1]
    step = pl.program_id(0)
    count = halves.shape[0]

    @pl.when(step == 0)
    def _():
        def prepare(c, carry):
            if turned_in:
                block = jnp.concatenate([f[c] for f in fields], axis=0).T
            elif blocked_in:
                block = fields[0][c]
            else:
                block = fields[0][:, pl.ds(pl.multiple_of(c * BLOCK, BLOCK), BLOCK)]
            high, low = split(block)
            halves[c, :rows] = high
            halves[c, rows:] = low
            return carry

        lax.fori_loop(0, count, prepare, 0, unroll=4)

    for i in range(per_step):
        base = (step * per_step + i) * slots
        gathered = jnp.concatenate([halves[cols[base + j]] for j in range(slots)], axis=1)
        factor = jnp.concatenate([factors[i, j] for j in range(slots)], axis=1)
        if turned_out:
            both = lax.dot_general(
                factor, gathered, (((1,), (1,)), ((), ())), preferred_element_type=jnp.float32
            )
            total = both[:, :rows] + both[:, rows:]
            size = BLOCK // len(outs)
            for q, out in enumerate(outs):
                out[i] = total[q * size : (q + 1) * size]
        else:
            both = lax.dot_general(
                gathered, factor, (((1,), (1,)), ((), ())), preferred_element_type=jnp.float32
            )
            total = both[:rows] + both[rows:]
            if len(outs[0].shape) == 3:
                outs[0][i] = total
            else:
                outs[0][:, i * BLOCK : (i + 1) * BLOCK] = total


def side(cols, fields, factors, form):
    blocks, slots = factors.shape[:2]
    per_step = ROWS_PER_STEP
    turned_in = tuple(fields) if form == "alpha_turned" else ()
    blocked_in = form == "alpha"
    if turned_in:
        rows = fields[0].shape[2]
    else:
        rows = fields[0].shape[1 if blocked_in else 0]
    if form == "beta_turned":
        size = BLOCK // CHUNKS
        out_shape = [jax.ShapeDtypeStruct((blocks, size, rows), jnp.float32)] * CHUNKS
        out_specs = [pl.BlockSpec((per_step, size, rows), lambda i, c: (i, 0, 0))] * CHUNKS
    elif form == "beta":
        out_shape = [jax.ShapeDtypeStruct((blocks, rows, BLOCK), jnp.float32)]
        out_specs = [pl.BlockSpec((per_step, rows, BLOCK), lambda i, c: (i, 0, 0))]
    else:
        out_shape = [jax.ShapeDtypeStruct((rows, blocks * BLOCK), jnp.float32)]
        out_specs = [pl.BlockSpec((rows, per_step * BLOCK), lambda i, c: (0, i))]
    in_specs = [
        pl.BlockSpec(f.shape, (lambda i, c: (0, 0, 0)) if len(f.shape) == 3 else (lambda i, c: (0, 0)))
        for f in fields
    ]
    in_specs.append(pl.BlockSpec((per_step, slots, BLOCK, BLOCK), lambda i, c: (i, 0, 0, 0)))
    return pl.pallas_call(
        functools.partial(
            side_kernel,
            blocked_in=blocked_in,
            turned_in=turned_in,
            turned_out=form == "beta_turned",
            rows=rows,
            slots=slots,
            per_step=per_step,
        ),
        out_shape=out_shape,
        grid_spec=pltpu.PrefetchScalarGridSpec(
            num_scalar_prefetch=1,
            grid=(blocks // per_step,),
            in_specs=in_specs,
            out_specs=out_specs,
            scratch_shapes=[pltpu.VMEM((blocks, 2 * rows, BLOCK), jnp.bfloat16)],
        ),
        compiler_params=pltpu.CompilerParams(vmem_limit_bytes=40 << 20),
        cost_estimate=pl.CostEstimate(
            flops=4 * rows * blocks * slots * BLOCK * BLOCK,
            bytes_accessed=factors.size * 2 + 8 * rows * blocks * BLOCK,
            transcendentals=0,
        ),
        name=form,
    )(cols, *fields, factors)


def turn_kernel(place, field, out, scratch):
    blocks, chunks, size = out.shape[:3]
    me = place[0]

    def one(c, carry):
        scratch[...] = field[:, pl.ds(pl.multiple_of(c * BLOCK, BLOCK), BLOCK)].T
        for q in range(chunks):
            start = pl.multiple_of(q * (BLOCK // chunks) + me * size, 8)
            out[c, q] = scratch[pl.ds(start, size)]
        return carry

    lax.fori_loop(0, blocks, one, 0, unroll=4)


def turned_share(field, shares):
    blocks = field.shape[1] // BLOCK
    size = BLOCK // CHUNKS // shares
    place = lax.axis_index("op").astype(jnp.int32).reshape(1)
    return pl.pallas_call(
        turn_kernel,
        out_shape=jax.ShapeDtypeStruct((blocks, CHUNKS, size, BLOCK), jnp.float32),
        in_specs=[
            pl.BlockSpec(memory_space=pltpu.SMEM),
            pl.BlockSpec(memory_space=pltpu.VMEM),
        ],
        out_specs=pl.BlockSpec(memory_space=pltpu.VMEM),
        scratch_shapes=[pltpu.VMEM((BLOCK, BLOCK), jnp.float32)],
        compiler_params=pltpu.CompilerParams(vmem_limit_bytes=40 << 20),
        name="turn",
    )(place, field)


def exchange(blocks, axis):
    return lax.all_to_all(blocks, axis, 0, 0, tiled=True)


def shared(part, shares):
    copies = jnp.broadcast_to(part[None], (shares, *part.shape))
    return exchange(copies, "op").reshape(-1, part.shape[-1])


def per_device(coeffs, previous, block_values, block_cols):
    shares = lax.axis_size("op")
    step_scale = 2.0 / math.sqrt(block_values.shape[0] * shares)
    width = coeffs.shape[1]
    factors = block_values[0]
    cols = block_cols[0].reshape(-1)
    me = lax.axis_index("op")

    def summed(partial):
        received = exchange(partial, "op").reshape(shares, -1, width)
        return jnp.sum(received, axis=0)

    parts = side(cols, [coeffs], factors, "beta_turned")
    before = exchange(turned_share(previous, shares), "str")
    sent = []
    for q in range(CHUNKS):
        (result,) = side(cols, [exchange(parts[q], "str")], factors, "alpha")
        earlier = before[:, q].transpose(1, 0, 2).reshape(-1, width)
        current = shared(step_scale * summed(result) - earlier, shares)
        (beta,) = side(cols, [current], factors, "beta")
        sent.append(exchange(beta, "str"))
    (result,) = side(cols, sent, factors, "alpha_turned")
    rows = coeffs.shape[0] // shares
    earlier = lax.dynamic_slice_in_dim(coeffs, me * rows, rows, 0)
    return shared(step_scale * summed(result) - earlier, shares)


def solution(mesh):
    placed = (P("str", None), P("str", None), P("op", None, None, None, None), P("op", None, None))
    return jax.shard_map(
        per_device, mesh=mesh, in_specs=placed, out_specs=P("str", None), check_vma=False
    )
```

```python
import functools
import math

import jax
import jax.numpy as jnp
from jax import lax
from jax.experimental import pallas as pl
from jax.experimental.pallas import tpu as pltpu
from jax.sharding import PartitionSpec as P

BLOCK = 128
GROUP = 8
VMEM_LIMIT = 56 << 20
ROWS_BY_ROWS = (((1,), (1,)), ((), ()))
ROWS_BY_COLUMNS = (((1,), (0,)), ((), ()))


def halves_of(values):
    high = values.astype(jnp.bfloat16)
    return high, (values - high.astype(jnp.float32)).astype(jnp.bfloat16)


def block_of(c):
    return pl.ds(pl.multiple_of(c * BLOCK, BLOCK), BLOCK)


def prepare(held, axis, fetch):
    def one(c, carry):
        held[c] = jnp.concatenate(halves_of(fetch(c)), axis=axis)
        return carry

    lax.fori_loop(0, held.shape[0], one, 0, unroll=4)


def picked(cols, held, r, axis):
    return jnp.concatenate([held[cols[0, r, j]] for j in range(cols.shape[2])], axis=axis)


def product(left, right, dims):
    return lax.dot_general(left, right, dims, preferred_element_type=jnp.float32)


def first_beta(cols, field, before, out, held):
    prepare(held, 0, lambda c: field[:, block_of(c)])

    def multiply(r, factor):
        both = product(factor, picked(cols, held, r, 1), ROWS_BY_ROWS)
        out[r, :BLOCK] = both[:, :BLOCK] + both[:, BLOCK:]
        out[r, BLOCK:] = before[:, block_of(r)]

    return multiply


def first_alpha(cols, field, out, held):
    prepare(held, 0, lambda c: field[c, :BLOCK])

    def multiply(r, factor):
        both = product(factor, picked(cols, held, r, 1), ROWS_BY_ROWS)
        total = both[:, :BLOCK] + both[:, BLOCK:]
        share = out.shape[2]
        for w in range(out.shape[0]):
            out[w, r] = total[w * share : (w + 1) * share]

    return multiply


def second_alpha(cols, field, out, held):
    prepare(held, 1, lambda c: jnp.concatenate([field[w, c] for w in range(field.shape[0])], axis=0))

    def multiply(r, factor):
        both = product(factor, picked(cols, held, r, 0), ROWS_BY_COLUMNS)
        out[r] = both[:, :BLOCK] + both[:, BLOCK:]

    return multiply


def second_beta(cols, field, out, held):
    prepare(held, 0, lambda c: field[c])

    def multiply(r, factor):
        both = product(picked(cols, held, r, 1), factor, ROWS_BY_ROWS)
        out[:, block_of(r)] = both[:BLOCK] + both[BLOCK:]

    return multiply


def with_factors(body, cols, factors, *refs):
    rest, local, landed = refs[:-2], refs[-2], refs[-1]
    groups, per_group, slots = local.shape[:3]

    def copy(g):
        return pltpu.make_async_copy(factors.at[0, pl.ds(g * per_group, per_group)], local.at[g], landed.at[g])

    for g in range(groups):
        copy(g).start()
    multiply = body(cols, *rest)

    def one(g, carry):
        copy(g).wait()
        for i in range(per_group):
            multiply(g * per_group + i, jnp.concatenate([local[g, i, j] for j in range(slots)], axis=1))
        return carry

    lax.fori_loop(0, groups, one, 0)


def side(body, cols, factors, fields, out, columns=False):
    blocks, slots = factors.shape[1:3]
    groups = blocks // GROUP
    in_vmem = pl.BlockSpec(memory_space=pltpu.VMEM)
    held = (blocks, BLOCK, 2 * BLOCK) if columns else (blocks, 2 * BLOCK, BLOCK)
    return pl.pallas_call(
        functools.partial(with_factors, body),
        out_shape=jax.ShapeDtypeStruct(out, jnp.float32),
        in_specs=[pl.BlockSpec(memory_space=pltpu.SMEM), pl.BlockSpec(memory_space=pl.ANY)]
        + [in_vmem] * len(fields),
        out_specs=in_vmem,
        scratch_shapes=[
            pltpu.VMEM(held, jnp.bfloat16),
            pltpu.VMEM((groups, GROUP, slots, BLOCK, BLOCK), jnp.bfloat16),
            pltpu.SemaphoreType.DMA((groups,)),
        ],
        compiler_params=pltpu.CompilerParams(vmem_limit_bytes=VMEM_LIMIT),
        cost_estimate=pl.CostEstimate(
            flops=4 * BLOCK * blocks * slots * BLOCK * BLOCK,
            bytes_accessed=factors.size * 2 + 8 * BLOCK * blocks * BLOCK,
            transcendentals=0,
        ),
        name=body.__name__,
    )(cols, factors, *fields)


def exchange(blocks, axis):
    return lax.all_to_all(blocks, axis, 0, 0, tiled=True)


def spread(piece, shares):
    return exchange(jnp.broadcast_to(piece[None], (shares, *piece.shape)), "op")


def per_device(coeffs, previous, block_values, block_cols):
    shares = lax.axis_size("op")
    step_scale = 2.0 / math.sqrt(block_values.shape[0] * shares)
    rows, width = coeffs.shape
    blocks = block_values.shape[1]
    share = rows // shares
    start = lax.axis_index("op") * share

    def own_rows(field):
        return lax.dynamic_slice_in_dim(field, start, share, 0)

    beta = side(
        first_beta, block_cols, block_values, [coeffs, own_rows(previous)], (blocks, rows + share, BLOCK)
    )
    received = exchange(beta, "str")
    part = side(first_alpha, block_cols, block_values, [received], (shares, blocks, share, BLOCK))
    total = jnp.sum(exchange(part, "op"), axis=0)
    current = spread(step_scale * total - received[:, rows:], shares)
    alpha = side(second_alpha, block_cols, block_values, [current], (blocks, rows, BLOCK), True)
    received = exchange(alpha, "str")
    part = side(second_beta, block_cols, block_values, [received], (rows, width))
    total = jnp.sum(exchange(part.reshape(shares, share, width), "op"), axis=0)
    return spread(step_scale * total - own_rows(coeffs), shares).reshape(rows, width)


def solution(mesh):
    placed = (P("str", None), P("str", None), P("op", None, None, None, None), P("op", None, None))
    return jax.shard_map(
        per_device, mesh=mesh, in_specs=placed, out_specs=P("str", None), check_vma=False
    )
```

```python
import functools
import math

import jax
import jax.numpy as jnp
from jax import lax
from jax.experimental import pallas as pl
from jax.experimental.pallas import tpu as pltpu
from jax.sharding import PartitionSpec as P

BLOCK = 128
GROUP = 8
VMEM_LIMIT = 56 << 20


def halves_of(values):
    high = values.astype(jnp.bfloat16)
    return high, (values - high.astype(jnp.float32)).astype(jnp.bfloat16)


def side_kernel(turn, write, cols, factors, field, *refs):
    extra, (out, held, blocks, fields, results, semaphores) = refs[:-6], refs[-6:]
    groups, per_group, slots = blocks.shape[:3]

    def read_field(g):
        if len(field.shape) == 2:
            part = field.at[:, pl.ds(g * per_group * BLOCK, per_group * BLOCK)]
        elif len(field.shape) == 3:
            part = field.at[pl.ds(g * per_group, per_group), :BLOCK]
        else:
            part = field.at[:, pl.ds(g * per_group, per_group)]
        return pltpu.make_async_copy(part, fields.at[g], semaphores.at[0, g])

    def read_factors(g):
        part = factors.at[0, pl.ds(g * per_group, per_group)]
        return pltpu.make_async_copy(part, blocks.at[g], semaphores.at[1, g])

    def write_out(g):
        if len(out.shape) == 2:
            part = out.at[:, pl.ds(pl.multiple_of(g * per_group * BLOCK, BLOCK), per_group * BLOCK)]
        elif len(out.shape) == 3:
            part = out.at[pl.ds(g * per_group, per_group)]
        else:
            part = out.at[:, pl.ds(g * per_group, per_group)]
        return pltpu.make_async_copy(results.at[g], part, semaphores.at[2, g])

    for g in range(groups):
        read_field(g).start()
    for g in range(groups):
        read_factors(g).start()
    for g in range(groups):
        read_field(g).wait()
        for i in range(per_group):
            if len(field.shape) == 2:
                block = fields[g, :, i * BLOCK : (i + 1) * BLOCK]
            elif len(field.shape) == 3:
                block = fields[g, i]
            else:
                block = jnp.concatenate([fields[g, w, i] for w in range(field.shape[0])], axis=0)
            if turn:
                block = block.T
            held[g * per_group + i] = jnp.concatenate(halves_of(block), axis=1)

    def one(g, carry):
        read_factors(g).wait()
        for i in range(per_group):
            r = g * per_group + i
            factor = jnp.concatenate([blocks[g, i, j] for j in range(slots)], axis=1)
            picked = jnp.concatenate([held[cols[j, 0, r]] for j in range(slots)], axis=0)
            both = jnp.dot(factor, picked, preferred_element_type=jnp.float32)
            write(results, g, i, r, both[:, :BLOCK] + both[:, BLOCK:], *extra)
        write_out(g).start()
        return carry

    lax.fori_loop(0, groups, one, 0)
    for g in range(groups):
        write_out(g).wait()


def write_block(results, g, i, r, total):
    results[g, i] = total


def write_with_share(results, g, i, r, total, before):
    results[g, i, :BLOCK] = total
    results[g, i, BLOCK:] = before[:, pl.ds(pl.multiple_of(r * BLOCK, BLOCK), BLOCK)]


def write_pieces(results, g, i, r, total):
    share = results.shape[3]
    for w in range(results.shape[1]):
        results[g, w, i] = total[w * share : (w + 1) * share]


def write_turned(results, g, i, r, total):
    results[g, :, i * BLOCK : (i + 1) * BLOCK] = total.T


def grouped(shape, groups):
    if len(shape) == 2:
        return (groups, shape[0], shape[1] // groups)
    if len(shape) == 3:
        return (groups, shape[0] // groups, *shape[1:])
    return (groups, shape[0], shape[1] // groups, *shape[2:])


def side(name, turn, write, cols, factors, field, out, *extra):
    blocks, slots = factors.shape[1:3]
    groups = blocks // GROUP
    anywhere = pl.BlockSpec(memory_space=pl.ANY)
    read = field.shape if len(field.shape) != 3 else (blocks, BLOCK, BLOCK)
    return pl.pallas_call(
        functools.partial(side_kernel, turn, write),
        out_shape=jax.ShapeDtypeStruct(out, jnp.float32),
        in_specs=[pl.BlockSpec(memory_space=pltpu.SMEM), anywhere, anywhere]
        + [pl.BlockSpec(memory_space=pltpu.VMEM)] * len(extra),
        out_specs=anywhere,
        scratch_shapes=[
            pltpu.VMEM((blocks, BLOCK, 2 * BLOCK), jnp.bfloat16),
            pltpu.VMEM((groups, GROUP, slots, BLOCK, BLOCK), jnp.bfloat16),
            pltpu.VMEM(grouped(read, groups), jnp.float32),
            pltpu.VMEM(grouped(out, groups), jnp.float32),
            pltpu.SemaphoreType.DMA((3, groups)),
        ],
        compiler_params=pltpu.CompilerParams(vmem_limit_bytes=VMEM_LIMIT),
        cost_estimate=pl.CostEstimate(
            flops=4 * BLOCK * blocks * slots * BLOCK * BLOCK,
            bytes_accessed=factors.size * 2 + 8 * BLOCK * blocks * BLOCK,
            transcendentals=0,
        ),
        name=name,
    )(cols, factors, field, *extra)


def exchange(blocks, axis):
    return lax.all_to_all(blocks, axis, 0, 0, tiled=True)


def spread(piece, shares):
    return exchange(jnp.broadcast_to(piece[None], (shares, *piece.shape)), "op")


def per_device(coeffs, previous, block_values, block_cols):
    shares = lax.axis_size("op")
    step_scale = 2.0 / math.sqrt(block_values.shape[0] * shares)
    rows, width = coeffs.shape
    blocks = block_values.shape[1]
    share = rows // shares
    start = lax.axis_index("op") * share

    def own_rows(field):
        return lax.dynamic_slice_in_dim(field, start, share, 0)

    def combined(parts, earlier):
        received = exchange(parts, "op")
        total = received[0]
        for w in range(1, shares):
            total = total + received[w]
        return spread(step_scale * total - earlier, shares)

    operators = (block_cols.transpose(2, 0, 1), block_values)
    sent = side(
        "first_right", True, write_with_share, *operators, coeffs, (blocks, rows + share, BLOCK), own_rows(previous)
    )
    received = exchange(sent, "str")
    parts = side("first_left", True, write_pieces, *operators, received, (shares, blocks, share, BLOCK))
    current = combined(parts, received[:, rows:])
    sent = side("second_left", False, write_block, *operators, current, (blocks, rows, BLOCK))
    received = exchange(sent, "str")
    parts = side("second_right", True, write_turned, *operators, received, (rows, width))
    return combined(parts.reshape(shares, share, width), own_rows(coeffs)).reshape(rows, width)


def solution(mesh):
    placed = (P("str", None), P("str", None), P("op", None, None, None, None), P("op", None, None))
    return jax.shard_map(
        per_device, mesh=mesh, in_specs=placed, out_specs=P("str", None), check_vma=False
    )
```

```python
import functools
import math

import jax
import jax.numpy as jnp
from jax import lax
from jax.experimental import pallas as pl
from jax.experimental.pallas import tpu as pltpu
from jax.sharding import PartitionSpec as P

BLOCK = 128
GROUP = 8
VMEM_LIMIT = 24 << 20


def halves_of(values):
    high = values.astype(jnp.bfloat16)
    return high, (values - high.astype(jnp.float32)).astype(jnp.bfloat16)


def side_kernel(turn, write, fill, cols, factors, field, *refs):
    extra, refs = refs[: len(refs) - (6 if fill else 5)], refs[len(refs) - (6 if fill else 5) :]
    if fill:
        out, table, held, fields, results, semaphores = refs
    else:
        table = factors
        out, held, fields, results, semaphores = refs
    groups = results.shape[0]
    blocks, slots = table.shape[:2]
    per_group = blocks // groups

    def read_field(g):
        if len(field.shape) == 2:
            part = field.at[:, pl.ds(g * per_group * BLOCK, per_group * BLOCK)]
        elif len(field.shape) == 3:
            part = field.at[pl.ds(g * per_group, per_group), :BLOCK]
        else:
            part = field.at[:, pl.ds(g * per_group, per_group)]
        return pltpu.make_async_copy(part, fields.at[g], semaphores.at[0, g])

    def read_factors(g):
        part = pl.ds(g * per_group, per_group)
        return pltpu.make_async_copy(factors.at[0, part], table.at[part], semaphores.at[1, g])

    def write_out(g):
        if len(out.shape) == 2:
            part = out.at[:, pl.ds(pl.multiple_of(g * per_group * BLOCK, BLOCK), per_group * BLOCK)]
        elif len(out.shape) == 3:
            part = out.at[pl.ds(g * per_group, per_group)]
        else:
            part = out.at[:, pl.ds(g * per_group, per_group)]
        return pltpu.make_async_copy(results.at[g], part, semaphores.at[2, g])

    for g in range(groups):
        read_field(g).start()
    if fill:
        for g in range(groups):
            read_factors(g).start()
    for g in range(groups):
        read_field(g).wait()
        for i in range(per_group):
            if len(field.shape) == 2:
                block = fields[g, :, i * BLOCK : (i + 1) * BLOCK]
            elif len(field.shape) == 3:
                block = fields[g, i]
            else:
                block = jnp.concatenate([fields[g, w, i] for w in range(field.shape[0])], axis=0)
            if turn:
                block = block.T
            held[g * per_group + i] = jnp.concatenate(halves_of(block), axis=1)

    def one(g, carry):
        if fill:
            read_factors(g).wait()
        for i in range(per_group):
            r = g * per_group + i
            factor = jnp.concatenate([table[r, j] for j in range(slots)], axis=1)
            picked = jnp.concatenate([held[cols[j, 0, r]] for j in range(slots)], axis=0)
            both = jnp.dot(factor, picked, preferred_element_type=jnp.float32)
            write(results, g, i, r, both[:, :BLOCK] + both[:, BLOCK:], *extra)
        write_out(g).start()
        return carry

    lax.fori_loop(0, groups, one, 0)
    for g in range(groups):
        write_out(g).wait()


def write_block(results, g, i, r, total):
    results[g, i] = total


def write_with_share(results, g, i, r, total, before):
    results[g, i, :BLOCK] = total
    results[g, i, BLOCK:] = before[:, pl.ds(pl.multiple_of(r * BLOCK, BLOCK), BLOCK)]


def write_pieces(results, g, i, r, total):
    share = results.shape[3]
    for w in range(results.shape[1]):
        results[g, w, i] = total[w * share : (w + 1) * share]


def write_turned(results, g, i, r, total):
    results[g, :, i * BLOCK : (i + 1) * BLOCK] = total.T


def grouped(shape, groups):
    if len(shape) == 2:
        return (groups, shape[0], shape[1] // groups)
    if len(shape) == 3:
        return (groups, shape[0] // groups, *shape[1:])
    return (groups, shape[0], shape[1] // groups, *shape[2:])


def side(name, turn, write, cols, factors, field, out, *extra):
    fill = len(factors.shape) == 5
    blocks, slots = factors.shape[-4:-2]
    groups = blocks // GROUP
    anywhere = pl.BlockSpec(memory_space=pl.ANY)
    in_vmem = pl.BlockSpec(memory_space=pltpu.VMEM)
    read = field.shape if len(field.shape) != 3 else (blocks, BLOCK, BLOCK)
    outs = [jax.ShapeDtypeStruct(out, jnp.float32)]
    if fill:
        outs.append(pltpu.VMEM((blocks, slots, BLOCK, BLOCK), jnp.bfloat16))
    return pl.pallas_call(
        functools.partial(side_kernel, turn, write, fill),
        out_shape=outs,
        in_specs=[pl.BlockSpec(memory_space=pltpu.SMEM), anywhere if fill else in_vmem, anywhere]
        + [in_vmem] * len(extra),
        out_specs=[anywhere, in_vmem][: len(outs)],
        scratch_shapes=[
            pltpu.VMEM((blocks, BLOCK, 2 * BLOCK), jnp.bfloat16),
            pltpu.VMEM(grouped(read, groups), jnp.float32),
            pltpu.VMEM(grouped(out, groups), jnp.float32),
            pltpu.SemaphoreType.DMA((3, groups)),
        ],
        compiler_params=pltpu.CompilerParams(vmem_limit_bytes=VMEM_LIMIT),
        cost_estimate=pl.CostEstimate(
            flops=4 * BLOCK * blocks * slots * BLOCK * BLOCK,
            bytes_accessed=factors.size * 2 + 8 * BLOCK * blocks * BLOCK,
            transcendentals=0,
        ),
        name=name,
    )(cols, factors, field, *extra)


def exchange(blocks, axis):
    return lax.all_to_all(blocks, axis, 0, 0, tiled=True)


def spread(piece, shares):
    return exchange(jnp.broadcast_to(piece[None], (shares, *piece.shape)), "op")


def per_device(coeffs, previous, block_values, block_cols):
    shares = lax.axis_size("op")
    step_scale = 2.0 / math.sqrt(block_values.shape[0] * shares)
    rows, width = coeffs.shape
    blocks = block_values.shape[1]
    share = rows // shares
    start = lax.axis_index("op") * share

    def own_rows(field):
        return lax.dynamic_slice_in_dim(field, start, share, 0)

    def combined(parts, earlier):
        received = exchange(parts, "op")
        total = received[0]
        for w in range(1, shares):
            total = total + received[w]
        return spread(step_scale * total - earlier, shares)

    cols = block_cols.transpose(2, 0, 1)
    sent, table = side(
        "first_right", True, write_with_share, cols, block_values, coeffs, (blocks, rows + share, BLOCK), own_rows(previous)
    )
    received = exchange(sent, "str")
    (parts,) = side("first_left", True, write_pieces, cols, table, received, (shares, blocks, share, BLOCK))
    current = combined(parts, received[:, rows:])
    (sent,) = side("second_left", False, write_block, cols, table, current, (blocks, rows, BLOCK))
    received = exchange(sent, "str")
    (parts,) = side("second_right", True, write_turned, cols, table, received, (rows, width))
    return combined(parts.reshape(shares, share, width), own_rows(coeffs)).reshape(rows, width)


def solution(mesh):
    placed = (P("str", None), P("str", None), P("op", None, None, None, None), P("op", None, None))
    return jax.shard_map(
        per_device, mesh=mesh, in_specs=placed, out_specs=P("str", None), check_vma=False
    )
```

```python
import functools
import math

import jax
import jax.numpy as jnp
from jax import lax
from jax.experimental import pallas as pl
from jax.experimental.pallas import tpu as pltpu
from jax.sharding import PartitionSpec as P

BLOCK = 128
GROUP = 8
VMEM_LIMIT = 24 << 20


def halves_of(values):
    high = values.astype(jnp.bfloat16)
    return high, (values - high.astype(jnp.float32)).astype(jnp.bfloat16)


def first_kernel(place, cols, factors, field, before, out, table, held, fields, share, results, landed):
    groups, per_group = results.shape[:2]
    rows = share.shape[0]

    def read_field(g):
        part = field.at[:, pl.ds(g * per_group * BLOCK, per_group * BLOCK)]
        return pltpu.make_async_copy(part, fields.at[g], landed.at[0, g])

    def read_factors(g):
        part = pl.ds(g * per_group, per_group)
        return pltpu.make_async_copy(factors.at[0, part], table.at[part], landed.at[1, g])

    def write_out(g):
        part = out.at[pl.ds(g * per_group, per_group)]
        return pltpu.make_async_copy(results.at[g], part, landed.at[2, g])

    start = pl.multiple_of(place[0] * rows, rows)
    read_before = pltpu.make_async_copy(before.at[pl.ds(start, rows)], share, landed.at[3, 0])
    for g in range(groups):
        read_field(g).start()
    read_before.start()
    for g in range(groups):
        read_factors(g).start()
    for g in range(groups):
        read_field(g).wait()
        for i in range(per_group):
            block = fields[g, :, i * BLOCK : (i + 1) * BLOCK]
            held[g * per_group + i] = jnp.concatenate(halves_of(block.T), axis=1)
    read_before.wait()

    def one(g, carry):
        read_factors(g).wait()
        for i in range(per_group):
            r = g * per_group + i
            results[g, i, :BLOCK] = product(cols, table, held, r)
            results[g, i, BLOCK:] = share[:, pl.ds(pl.multiple_of(r * BLOCK, BLOCK), BLOCK)]
        write_out(g).start()
        return carry

    lax.fori_loop(0, groups, one, 0)
    for g in range(groups):
        write_out(g).wait()


def product(cols, table, held, r):
    slots = table.shape[1]
    factor = jnp.concatenate([table[r, j] for j in range(slots)], axis=1)
    picked = jnp.concatenate([held[cols[j, 0, r]] for j in range(slots)], axis=0)
    both = jnp.dot(factor, picked, preferred_element_type=jnp.float32)
    return both[:, :BLOCK] + both[:, BLOCK:]


def later_kernel(read, write, cols, table, field, out, held):
    blocks = table.shape[0]
    for c in range(blocks):
        held[c] = jnp.concatenate(halves_of(read(field, c)), axis=1)

    def one(g, carry):
        for i in range(GROUP):
            r = g * GROUP + i
            write(out, r, product(cols, table, held, r))
        return carry

    lax.fori_loop(0, blocks // GROUP, one, 0)


def read_turned(field, c):
    return field[c, :BLOCK].T


def read_pieces(field, c):
    return jnp.concatenate([field[w, c] for w in range(field.shape[0])], axis=0)


def write_block(out, r, total):
    out[r] = total


def write_pieces(out, r, total):
    share = out.shape[2]
    for w in range(out.shape[0]):
        out[w, r] = total[w * share : (w + 1) * share]


def write_turned(out, r, total):
    out[:, pl.ds(pl.multiple_of(r * BLOCK, BLOCK), BLOCK)] = total.T


def cost(blocks, slots):
    size = blocks * BLOCK * BLOCK
    return pl.CostEstimate(flops=4 * size * slots * BLOCK, bytes_accessed=size * (2 * slots + 8), transcendentals=0)


def first_side(place, cols, factors, field, before, share):
    blocks, slots = factors.shape[1:3]
    groups = blocks // GROUP
    rows = field.shape[0]
    in_smem, in_vmem, in_hbm = (pl.BlockSpec(memory_space=m) for m in (pltpu.SMEM, pltpu.VMEM, pltpu.HBM))
    far = [pltpu.with_memory_space_constraint(x, pltpu.HBM) for x in (factors, field, before)]
    return pl.pallas_call(
        first_kernel,
        out_shape=[
            jax.ShapeDtypeStruct((blocks, rows + share, BLOCK), jnp.float32),
            pltpu.VMEM((blocks, slots, BLOCK, BLOCK), jnp.bfloat16),
        ],
        in_specs=[in_smem, in_smem, in_hbm, in_hbm, in_hbm],
        out_specs=[pl.BlockSpec(memory_space=pl.ANY), in_vmem],
        scratch_shapes=[
            pltpu.VMEM((blocks, BLOCK, 2 * BLOCK), jnp.bfloat16),
            pltpu.VMEM((groups, rows, GROUP * BLOCK), jnp.float32),
            pltpu.VMEM((share, blocks * BLOCK), jnp.float32),
            pltpu.VMEM((groups, GROUP, rows + share, BLOCK), jnp.float32),
            pltpu.SemaphoreType.DMA((4, groups)),
        ],
        compiler_params=pltpu.CompilerParams(vmem_limit_bytes=VMEM_LIMIT),
        cost_estimate=cost(blocks, slots),
        name="first_right",
    )(place, cols, *far)


def side(name, read, write, cols, table, field, out):
    blocks, slots = table.shape[:2]
    in_vmem = pl.BlockSpec(memory_space=pltpu.VMEM)
    return pl.pallas_call(
        functools.partial(later_kernel, read, write),
        out_shape=pltpu.VMEM(out, jnp.float32),
        in_specs=[pl.BlockSpec(memory_space=pltpu.SMEM), in_vmem, in_vmem],
        out_specs=in_vmem,
        scratch_shapes=[pltpu.VMEM((blocks, BLOCK, 2 * BLOCK), jnp.bfloat16)],
        compiler_params=pltpu.CompilerParams(vmem_limit_bytes=VMEM_LIMIT),
        cost_estimate=cost(blocks, slots),
        name=name,
    )(cols, table, pltpu.with_memory_space_constraint(field, pltpu.VMEM))


def exchange(blocks, axis):
    return lax.all_to_all(blocks, axis, 0, 0, tiled=True)


def spread(piece, shares):
    return exchange(jnp.broadcast_to(piece[None], (shares, *piece.shape)), "op")


def per_device(coeffs, previous, block_values, block_cols):
    shares = lax.axis_size("op")
    step_scale = 2.0 / math.sqrt(block_values.shape[0] * shares)
    rows, width = coeffs.shape
    blocks = block_values.shape[1]
    share = rows // shares
    start = lax.axis_index("op") * share

    def own_rows(field):
        return lax.dynamic_slice_in_dim(field, start, share, 0)

    def combined(parts, earlier):
        received = exchange(parts, "op")
        total = received[0]
        for w in range(1, shares):
            total = total + received[w]
        return spread(step_scale * total - earlier, shares)

    cols = block_cols.transpose(2, 0, 1)
    place = lax.axis_index("op").astype(jnp.int32).reshape(1)
    sent, table = first_side(place, cols, block_values, coeffs, previous, share)
    received = exchange(sent, "str")
    parts = side("first_left", read_turned, write_pieces, cols, table, received, (shares, blocks, share, BLOCK))
    current = combined(parts, received[:, rows:])
    sent = side("second_left", read_pieces, write_block, cols, table, current, (blocks, rows, BLOCK))
    received = exchange(sent, "str")
    parts = side("second_right", read_turned, write_turned, cols, table, received, (rows, width))
    return combined(parts.reshape(shares, share, width), own_rows(coeffs)).reshape(rows, width)


def solution(mesh):
    placed = (P("str", None), P("str", None), P("op", None, None, None, None), P("op", None, None))
    return jax.shard_map(
        per_device, mesh=mesh, in_specs=placed, out_specs=P("str", None), check_vma=False
    )
```

```python
import functools
import math

import jax
import jax.numpy as jnp
from jax import lax
from jax.experimental import pallas as pl
from jax.experimental.pallas import tpu as pltpu
from jax.sharding import PartitionSpec as P

BLOCK = 128
GROUP = 8
VMEM_LIMIT = 24 << 20


def halves_of(values):
    high = values.astype(jnp.bfloat16)
    return high, (values - high.astype(jnp.float32)).astype(jnp.bfloat16)


def first_kernel(place, cols, factors, field, before, out, table, kept, held, fields, share, results, landed):
    groups, per_group = results.shape[:2]
    rows = share.shape[0]

    def read_field(g):
        part = field.at[:, pl.ds(g * per_group * BLOCK, per_group * BLOCK)]
        return pltpu.make_async_copy(part, fields.at[g], landed.at[0, g])

    def read_factors(g):
        part = pl.ds(g * per_group, per_group)
        return pltpu.make_async_copy(factors.at[0, part], table.at[part], landed.at[1, g])

    def write_out(g):
        part = out.at[pl.ds(g * per_group, per_group)]
        return pltpu.make_async_copy(results.at[g], part, landed.at[2, g])

    start = pl.multiple_of(place[0] * rows, rows)
    read_before = pltpu.make_async_copy(before.at[pl.ds(start, rows)], share, landed.at[3, 0])
    for g in range(groups):
        read_field(g).start()
    read_before.start()
    for g in range(groups):
        read_factors(g).start()
    for g in range(groups):
        read_field(g).wait()
        kept[:, g * per_group * BLOCK : (g + 1) * per_group * BLOCK] = fields[g, pl.ds(start, rows)]
        for i in range(per_group):
            block = fields[g, :, i * BLOCK : (i + 1) * BLOCK]
            held[g * per_group + i] = jnp.concatenate(halves_of(block.T), axis=1)
    read_before.wait()

    def one(g, carry):
        read_factors(g).wait()
        for i in range(per_group):
            r = g * per_group + i
            results[g, i, :BLOCK] = product(cols, table, held, r)
            results[g, i, BLOCK:] = share[:, pl.ds(pl.multiple_of(r * BLOCK, BLOCK), BLOCK)]
        write_out(g).start()
        return carry

    lax.fori_loop(0, groups, one, 0)
    for g in range(groups):
        write_out(g).wait()


def product(cols, table, held, r):
    slots = table.shape[1]
    factor = jnp.concatenate([table[r, j] for j in range(slots)], axis=1)
    picked = jnp.concatenate([held[cols[j, 0, r]] for j in range(slots)], axis=0)
    both = jnp.dot(factor, picked, preferred_element_type=jnp.float32)
    return both[:, :BLOCK] + both[:, BLOCK:]


def later_kernel(read, write, cols, table, field, out, held):
    blocks = table.shape[0]
    for c in range(blocks):
        held[c] = jnp.concatenate(halves_of(read(field, c)), axis=1)

    def one(g, carry):
        for i in range(GROUP):
            r = g * GROUP + i
            write(out, r, product(cols, table, held, r))
        return carry

    lax.fori_loop(0, blocks // GROUP, one, 0)


def read_turned(field, c):
    return field[c, :BLOCK].T


def read_pieces(field, c):
    return jnp.concatenate([field[w, c] for w in range(field.shape[0])], axis=0)


def write_block(out, r, total):
    out[r] = total


def write_pieces(out, r, total):
    share = out.shape[2]
    for w in range(out.shape[0]):
        out[w, r] = total[w * share : (w + 1) * share]


def write_turned(out, r, total):
    out[:, pl.ds(pl.multiple_of(r * BLOCK, BLOCK), BLOCK)] = total.T


def cost(blocks, slots):
    size = blocks * BLOCK * BLOCK
    return pl.CostEstimate(flops=4 * size * slots * BLOCK, bytes_accessed=size * (2 * slots + 8), transcendentals=0)


def first_side(place, cols, factors, field, before, share):
    blocks, slots = factors.shape[1:3]
    groups = blocks // GROUP
    rows = field.shape[0]
    in_smem, in_vmem, in_hbm = (pl.BlockSpec(memory_space=m) for m in (pltpu.SMEM, pltpu.VMEM, pltpu.HBM))
    far = [pltpu.with_memory_space_constraint(x, pltpu.HBM) for x in (factors, field, before)]
    return pl.pallas_call(
        first_kernel,
        out_shape=[
            jax.ShapeDtypeStruct((blocks, rows + share, BLOCK), jnp.float32),
            pltpu.VMEM((blocks, slots, BLOCK, BLOCK), jnp.bfloat16),
            pltpu.VMEM((share, blocks * BLOCK), jnp.float32),
        ],
        in_specs=[in_smem, in_smem, in_hbm, in_hbm, in_hbm],
        out_specs=[pl.BlockSpec(memory_space=pl.ANY), in_vmem, in_vmem],
        scratch_shapes=[
            pltpu.VMEM((blocks, BLOCK, 2 * BLOCK), jnp.bfloat16),
            pltpu.VMEM((groups, rows, GROUP * BLOCK), jnp.float32),
            pltpu.VMEM((share, blocks * BLOCK), jnp.float32),
            pltpu.VMEM((groups, GROUP, rows + share, BLOCK), jnp.float32),
            pltpu.SemaphoreType.DMA((4, groups)),
        ],
        compiler_params=pltpu.CompilerParams(vmem_limit_bytes=VMEM_LIMIT),
        cost_estimate=cost(blocks, slots),
        name="first_right",
    )(place, cols, *far)


def side(name, read, write, cols, table, field, out):
    blocks, slots = table.shape[:2]
    in_vmem = pl.BlockSpec(memory_space=pltpu.VMEM)
    return pl.pallas_call(
        functools.partial(later_kernel, read, write),
        out_shape=pltpu.VMEM(out, jnp.float32),
        in_specs=[pl.BlockSpec(memory_space=pltpu.SMEM), in_vmem, in_vmem],
        out_specs=in_vmem,
        scratch_shapes=[pltpu.VMEM((blocks, BLOCK, 2 * BLOCK), jnp.bfloat16)],
        compiler_params=pltpu.CompilerParams(vmem_limit_bytes=VMEM_LIMIT),
        cost_estimate=cost(blocks, slots),
        name=name,
    )(cols, table, pltpu.with_memory_space_constraint(field, pltpu.VMEM))


def exchange(blocks, axis):
    return lax.all_to_all(blocks, axis, 0, 0, tiled=True)


def spread(piece, shares):
    return exchange(jnp.broadcast_to(piece[None], (shares, *piece.shape)), "op")


def per_device(coeffs, previous, block_values, block_cols):
    shares = lax.axis_size("op")
    step_scale = 2.0 / math.sqrt(block_values.shape[0] * shares)
    rows, width = coeffs.shape
    blocks = block_values.shape[1]
    share = rows // shares

    def combined(parts, earlier):
        received = exchange(parts, "op")
        total = received[0]
        for w in range(1, shares):
            total = total + received[w]
        return spread(step_scale * total - earlier, shares)

    cols = block_cols.transpose(2, 0, 1)
    place = lax.axis_index("op").astype(jnp.int32).reshape(1)
    sent, table, kept = first_side(place, cols, block_values, coeffs, previous, share)
    received = exchange(sent, "str")
    parts = side("first_left", read_turned, write_pieces, cols, table, received, (shares, blocks, share, BLOCK))
    current = combined(parts, received[:, rows:])
    sent = side("second_left", read_pieces, write_block, cols, table, current, (blocks, rows, BLOCK))
    received = exchange(sent, "str")
    parts = side("second_right", read_turned, write_turned, cols, table, received, (rows, width))
    return combined(parts.reshape(shares, share, width), kept).reshape(rows, width)


def solution(mesh):
    placed = (P("str", None), P("str", None), P("op", None, None, None, None), P("op", None, None))
    return jax.shard_map(
        per_device, mesh=mesh, in_specs=placed, out_specs=P("str", None), check_vma=False
    )
```

```python
import functools
import math

import jax
import jax.numpy as jnp
from jax import lax
from jax.experimental import pallas as pl
from jax.experimental.pallas import tpu as pltpu
from jax.sharding import PartitionSpec as P

BLOCK = 128
GROUP = 8
VMEM_LIMIT = 24 << 20


def halves_of(values):
    high = values.astype(jnp.bfloat16)
    return high, (values - high.astype(jnp.float32)).astype(jnp.bfloat16)


def first_kernel(place, columns, factors, field, before, out, table, kept, cols, held, fields, share, landed):
    groups = fields.shape[0]
    per_group = table.shape[0] // groups
    rows = share.shape[0]

    def read_field(g):
        part = field.at[:, pl.ds(g * per_group * BLOCK, per_group * BLOCK)]
        return pltpu.make_async_copy(part, fields.at[g], landed.at[0, g])

    def read_factors(g):
        part = pl.ds(g * per_group, per_group)
        return pltpu.make_async_copy(factors.at[0, part], table.at[part], landed.at[1, g])

    start = pl.multiple_of(place[0] * rows, rows)
    read_before = pltpu.make_async_copy(before.at[pl.ds(start, rows)], share, landed.at[2, 0])
    read_columns = pltpu.make_async_copy(columns, cols, landed.at[2, 1])
    for g in range(groups):
        read_field(g).start()
    read_columns.start()
    read_before.start()
    for g in range(groups):
        read_factors(g).start()
    for g in range(groups):
        read_field(g).wait()
        kept[:, g * per_group * BLOCK : (g + 1) * per_group * BLOCK] = fields[g, pl.ds(start, rows)]
        for i in range(per_group):
            block = fields[g, :, i * BLOCK : (i + 1) * BLOCK]
            held[g * per_group + i] = jnp.concatenate(halves_of(block.T), axis=1)
    read_columns.wait()
    read_before.wait()

    def one(g, carry):
        read_factors(g).wait()
        for i in range(per_group):
            r = g * per_group + i
            out[r, :BLOCK] = product(cols, table, held, r)
            out[r, BLOCK:] = share[:, pl.ds(pl.multiple_of(r * BLOCK, BLOCK), BLOCK)]
        return carry

    lax.fori_loop(0, groups, one, 0)


def product(cols, table, held, r):
    slots = table.shape[1]
    factor = jnp.concatenate([table[r, j] for j in range(slots)], axis=1)
    picked = jnp.concatenate([held[cols[j, 0, r]] for j in range(slots)], axis=0)
    both = jnp.dot(factor, picked, preferred_element_type=jnp.float32)
    return both[:, :BLOCK] + both[:, BLOCK:]


def later_kernel(read, write, cols, table, field, out, held):
    blocks = table.shape[0]
    for c in range(blocks):
        held[c] = jnp.concatenate(halves_of(read(field, c)), axis=1)

    def one(g, carry):
        for i in range(GROUP):
            r = g * GROUP + i
            write(out, r, product(cols, table, held, r))
        return carry

    lax.fori_loop(0, blocks // GROUP, one, 0)


def read_turned(field, c):
    return field[c, :BLOCK].T


def read_pieces(field, c):
    return jnp.concatenate([field[w, c] for w in range(field.shape[0])], axis=0)


def write_block(out, r, total):
    out[r] = total


def write_pieces(out, r, total):
    share = out.shape[2]
    for w in range(out.shape[0]):
        out[w, r] = total[w * share : (w + 1) * share]


def write_turned(out, r, total):
    out[:, pl.ds(pl.multiple_of(r * BLOCK, BLOCK), BLOCK)] = total.T


def cost(blocks, slots):
    size = blocks * BLOCK * BLOCK
    return pl.CostEstimate(flops=4 * size * slots * BLOCK, bytes_accessed=size * (2 * slots + 8), transcendentals=0)


def first_side(place, cols, factors, field, before, share):
    blocks, slots = factors.shape[1:3]
    groups = blocks // GROUP
    rows = field.shape[0]
    in_smem, in_vmem, in_hbm = (pl.BlockSpec(memory_space=m) for m in (pltpu.SMEM, pltpu.VMEM, pltpu.HBM))
    far = [pltpu.with_memory_space_constraint(x, pltpu.HBM) for x in (cols, factors, field, before)]
    return pl.pallas_call(
        first_kernel,
        out_shape=[
            pltpu.VMEM((blocks, rows + share, BLOCK), jnp.float32),
            pltpu.VMEM((blocks, slots, BLOCK, BLOCK), jnp.bfloat16),
            pltpu.VMEM((share, blocks * BLOCK), jnp.float32),
        ],
        in_specs=[in_smem] + [in_hbm] * 4,
        out_specs=[in_vmem] * 3,
        scratch_shapes=[
            pltpu.SMEM(cols.shape, jnp.int32),
            pltpu.VMEM((blocks, BLOCK, 2 * BLOCK), jnp.bfloat16),
            pltpu.VMEM((groups, rows, GROUP * BLOCK), jnp.float32),
            pltpu.VMEM((share, blocks * BLOCK), jnp.float32),
            pltpu.SemaphoreType.DMA((3, groups)),
        ],
        compiler_params=pltpu.CompilerParams(vmem_limit_bytes=VMEM_LIMIT),
        cost_estimate=cost(blocks, slots),
        name="first_right",
    )(place, *far)


def side(name, read, write, cols, table, field, out):
    blocks, slots = table.shape[:2]
    in_vmem = pl.BlockSpec(memory_space=pltpu.VMEM)
    return pl.pallas_call(
        functools.partial(later_kernel, read, write),
        out_shape=pltpu.VMEM(out, jnp.float32),
        in_specs=[pl.BlockSpec(memory_space=pltpu.SMEM), in_vmem, in_vmem],
        out_specs=in_vmem,
        scratch_shapes=[pltpu.VMEM((blocks, BLOCK, 2 * BLOCK), jnp.bfloat16)],
        compiler_params=pltpu.CompilerParams(vmem_limit_bytes=VMEM_LIMIT),
        cost_estimate=cost(blocks, slots),
        name=name,
    )(cols, table, pltpu.with_memory_space_constraint(field, pltpu.VMEM))


def exchange(blocks, axis):
    return lax.all_to_all(blocks, axis, 0, 0, tiled=True)


def spread(piece, shares):
    return exchange(jnp.broadcast_to(piece[None], (shares, *piece.shape)), "op")


def per_device(coeffs, previous, block_values, block_cols):
    shares = lax.axis_size("op")
    step_scale = 2.0 / math.sqrt(block_values.shape[0] * shares)
    rows, width = coeffs.shape
    blocks = block_values.shape[1]
    share = rows // shares

    def combined(parts, earlier):
        received = exchange(parts, "op")
        total = received[0]
        for w in range(1, shares):
            total = total + received[w]
        return spread(step_scale * total - earlier, shares)

    cols = block_cols.transpose(2, 0, 1)
    place = lax.axis_index("op").astype(jnp.int32).reshape(1)
    sent, table, kept = first_side(place, cols, block_values, coeffs, previous, share)
    received = exchange(sent, "str")
    parts = side("first_left", read_turned, write_pieces, cols, table, received, (shares, blocks, share, BLOCK))
    current = combined(parts, received[:, rows:])
    sent = side("second_left", read_pieces, write_block, cols, table, current, (blocks, rows, BLOCK))
    received = exchange(sent, "str")
    parts = side("second_right", read_turned, write_turned, cols, table, received, (rows, width))
    return combined(parts.reshape(shares, share, width), kept).reshape(rows, width)


def solution(mesh):
    placed = (P("str", None), P("str", None), P("op", None, None, None, None), P("op", None, None))
    return jax.shard_map(
        per_device, mesh=mesh, in_specs=placed, out_specs=P("str", None), check_vma=False
    )
```

```python
import functools
import math

import jax
import jax.numpy as jnp
from jax import lax
from jax.experimental import pallas as pl
from jax.experimental.pallas import tpu as pltpu
from jax.sharding import PartitionSpec as P

BLOCK = 128
GROUP = 8
VMEM_LIMIT = 24 << 20


def halves_of(values):
    high = values.astype(jnp.bfloat16)
    return high, (values - high.astype(jnp.float32)).astype(jnp.bfloat16)


def first_kernel(place, columns, factors, field, before, out, table, kept, cols, held, fields, share, landed):
    groups = fields.shape[0]
    per_group = table.shape[0] // groups
    rows = share.shape[0]

    def read_field(g):
        part = field.at[:, pl.ds(g * per_group * BLOCK, per_group * BLOCK)]
        return pltpu.make_async_copy(part, fields.at[g], landed.at[0, g])

    def read_factors(g):
        part = pl.ds(g * per_group, per_group)
        return pltpu.make_async_copy(factors.at[0, part], table.at[part], landed.at[1, g])

    start = pl.multiple_of(place[0] * rows, rows)
    read_before = pltpu.make_async_copy(before.at[pl.ds(start, rows)], share, landed.at[2, 0])
    read_columns = pltpu.make_async_copy(columns, cols, landed.at[2, 1])
    for g in range(groups):
        read_field(g).start()
    read_columns.start()
    read_before.start()
    for g in range(groups):
        read_factors(g).start()
    for g in range(groups):
        read_field(g).wait()
        kept[:, g * per_group * BLOCK : (g + 1) * per_group * BLOCK] = fields[g, pl.ds(start, rows)]
        for i in range(per_group):
            block = fields[g, :, i * BLOCK : (i + 1) * BLOCK]
            held[g * per_group + i] = jnp.concatenate(halves_of(block.T), axis=1)
    read_columns.wait()
    read_before.wait()

    def one(g, carry):
        read_factors(g).wait()
        for i in range(per_group):
            r = g * per_group + i
            out[r, :BLOCK] = product(cols, table, held, r)
            out[r, BLOCK:] = share[:, pl.ds(pl.multiple_of(r * BLOCK, BLOCK), BLOCK)]
        return carry

    lax.fori_loop(0, groups, one, 0)


def product(cols, table, held, r):
    slots = table.shape[1]
    factor = jnp.concatenate([table[r, j] for j in range(slots)], axis=1)
    picked = jnp.concatenate([held[cols[j, 0, r]] for j in range(slots)], axis=0)
    both = jnp.dot(factor, picked, preferred_element_type=jnp.float32)
    return both[:, :BLOCK] + both[:, BLOCK:]


def later_kernel(read, write, cols, table, field, out, held):
    blocks = table.shape[0]
    for c in range(blocks):
        held[c] = jnp.concatenate(halves_of(read(field, c)), axis=1)

    for r in range(blocks):
        write(out, r, product(cols, table, held, r))


def read_turned(field, c):
    return field[c, :BLOCK].T


def read_pieces(field, c):
    return jnp.concatenate([field[w, c] for w in range(field.shape[0])], axis=0)


def write_block(out, r, total):
    out[r] = total


def write_pieces(out, r, total):
    share = out.shape[2]
    for w in range(out.shape[0]):
        out[w, r] = total[w * share : (w + 1) * share]


def write_turned(out, r, total):
    out[:, r * BLOCK : (r + 1) * BLOCK] = total.T


def cost(blocks, slots):
    size = blocks * BLOCK * BLOCK
    return pl.CostEstimate(flops=4 * size * slots * BLOCK, bytes_accessed=size * (2 * slots + 8), transcendentals=0)


def first_side(place, cols, factors, field, before, share):
    blocks, slots = factors.shape[1:3]
    groups = blocks // GROUP
    rows = field.shape[0]
    in_smem, in_vmem, in_hbm = (pl.BlockSpec(memory_space=m) for m in (pltpu.SMEM, pltpu.VMEM, pltpu.HBM))
    far = [pltpu.with_memory_space_constraint(x, pltpu.HBM) for x in (cols, factors, field, before)]
    return pl.pallas_call(
        first_kernel,
        out_shape=[
            pltpu.VMEM((blocks, rows + share, BLOCK), jnp.float32),
            pltpu.VMEM((blocks, slots, BLOCK, BLOCK), jnp.bfloat16),
            pltpu.VMEM((share, blocks * BLOCK), jnp.float32),
        ],
        in_specs=[in_smem] + [in_hbm] * 4,
        out_specs=[in_vmem] * 3,
        scratch_shapes=[
            pltpu.SMEM(cols.shape, jnp.int32),
            pltpu.VMEM((blocks, BLOCK, 2 * BLOCK), jnp.bfloat16),
            pltpu.VMEM((groups, rows, GROUP * BLOCK), jnp.float32),
            pltpu.VMEM((share, blocks * BLOCK), jnp.float32),
            pltpu.SemaphoreType.DMA((3, groups)),
        ],
        compiler_params=pltpu.CompilerParams(vmem_limit_bytes=VMEM_LIMIT),
        cost_estimate=cost(blocks, slots),
        name="first_right",
    )(place, *far)


def side(name, read, write, cols, table, field, out):
    blocks, slots = table.shape[:2]
    in_vmem = pl.BlockSpec(memory_space=pltpu.VMEM)
    return pl.pallas_call(
        functools.partial(later_kernel, read, write),
        out_shape=pltpu.VMEM(out, jnp.float32),
        in_specs=[pl.BlockSpec(memory_space=pltpu.SMEM), in_vmem, in_vmem],
        out_specs=in_vmem,
        scratch_shapes=[pltpu.VMEM((blocks, BLOCK, 2 * BLOCK), jnp.bfloat16)],
        compiler_params=pltpu.CompilerParams(vmem_limit_bytes=VMEM_LIMIT),
        cost_estimate=cost(blocks, slots),
        name=name,
    )(cols, table, pltpu.with_memory_space_constraint(field, pltpu.VMEM))


def exchange(blocks, axis):
    return lax.all_to_all(blocks, axis, 0, 0, tiled=True)


def spread(piece, shares):
    return exchange(jnp.broadcast_to(piece[None], (shares, *piece.shape)), "op")


def per_device(coeffs, previous, block_values, block_cols):
    shares = lax.axis_size("op")
    step_scale = 2.0 / math.sqrt(block_values.shape[0] * shares)
    rows, width = coeffs.shape
    blocks = block_values.shape[1]
    share = rows // shares

    def combined(parts, earlier):
        received = exchange(parts, "op")
        total = received[0]
        for w in range(1, shares):
            total = total + received[w]
        return spread(step_scale * total - earlier, shares)

    cols = block_cols.transpose(2, 0, 1)
    place = lax.axis_index("op").astype(jnp.int32).reshape(1)
    sent, table, kept = first_side(place, cols, block_values, coeffs, previous, share)
    received = exchange(sent, "str")
    parts = side("first_left", read_turned, write_pieces, cols, table, received, (shares, blocks, share, BLOCK))
    current = combined(parts, received[:, rows:])
    sent = side("second_left", read_pieces, write_block, cols, table, current, (blocks, rows, BLOCK))
    received = exchange(sent, "str")
    parts = side("second_right", read_turned, write_turned, cols, table, received, (rows, width))
    return combined(parts.reshape(shares, share, width), kept).reshape(rows, width)


def solution(mesh):
    placed = (P("str", None), P("str", None), P("op", None, None, None, None), P("op", None, None))
    return jax.shard_map(
        per_device, mesh=mesh, in_specs=placed, out_specs=P("str", None), check_vma=False
    )
```
